32 devices in a mesh: blk: 8 (over y, x, core), off: 4 (over z).
Axes of the slice: x: 2, y: 2, z: 4, core: 2. Of those that a mesh axis runs over, the one named last changes fastest.
Arguments:
- coefficients: bfloat16 [128, 32, 128], P('blk', 'off'), may hold values from -12 to 12
Outputs:
- smoothed: float32 [128, 32, 128], P(('blk', 'off'))
- log_degree: float32 [128], P(('blk', 'off'))
The draws below stay inside these ranges and needn't reach their ends.
All inputs are finite; a program needn't handle non-finite values.
Results may differ from the reference program's by a relative error of at most 0.005.
Values may be sent and summed in bfloat16 or wider, within the bound.
No kernel may reach another device: no remote copies, remote signals or barrier semaphores. Data moves between devices by JAX's collectives and lax.ppermute only.
A program may use at most 64 MiB of HBM per device.

```python
import math
import jax
import jax.numpy as jnp
from jax import lax

R = 32
A = 128
BLK = 16
NIMG = 128
NCLASS = 8
WINDOW = 8


def draw_coefficients(key, part):
    base_key = jax.random.fold_in(key, 7)
    template_key, label_key, angle_key, noise_key = jax.random.split(base_key, 4)
    half_width = A // 2
    noise_level = 1.6
    templates = jax.random.truncated_normal(template_key, -4.0, 4.0, (NCLASS, R, A), jnp.float32)
    labels = jax.random.randint(label_key, (NIMG,), 0, NCLASS)
    angles = jax.random.uniform(angle_key, (NIMG,), jnp.float32, 0.0, 2.0 * math.pi)
    noise = noise_level * jax.random.truncated_normal(noise_key, -4.0, 4.0, (NIMG, R, A), jnp.float32)
    picked = templates[labels]
    frequency = jnp.arange(half_width, dtype=jnp.float32)
    phase = angles[:, None] * frequency[None, :]
    cos_phase = jnp.cos(phase)[:, None, :]
    sin_phase = jnp.sin(phase)[:, None, :]
    real_part = picked[:, :, :half_width]
    imag_part = picked[:, :, half_width:]
    rotated_real = real_part * cos_phase + imag_part * sin_phase
    rotated_imag = imag_part * cos_phase - real_part * sin_phase
    rotated = jnp.concatenate([rotated_real, rotated_imag], axis=2)
    return (rotated + noise).astype(jnp.bfloat16)


def setup_inputs(seed: int = 0) -> dict:
    key_of = jax.random.split(jax.random.key(seed), 2)
    return {
        "coefficients": draw_coefficients(jax.random.fold_in(key_of[1], 71), 0),
    }


epsilon = 1e-06
concentration = 40.0

def angle_tables(angular):
    half_width = angular // 2
    frequency = jnp.arange(half_width, dtype=jnp.int32)
    shifts = jnp.arange(angular, dtype=jnp.int32)
    product = frequency[:, None] * shifts[None, :] % angular
    phase = product.astype(jnp.float32) * (2.0 * math.pi / angular)
    forward = jnp.concatenate([jnp.cos(phase), -jnp.sin(phase)], axis=0)
    return forward

def reference(coefficients):
    half_width = A // 2
    forward = angle_tables(A)
    backward = forward.T
    values = coefficients.astype(jnp.float32)
    inverse_norm = lax.rsqrt(lax.optimization_barrier(jnp.sum(values * values, axis=(1, 2))) + epsilon)
    swapped = jnp.concatenate([values[:, :, half_width:], values[:, :, :half_width]], axis=2)
    block_count = NIMG // BLK
    block_numbers = jnp.arange(block_count, dtype=jnp.int32)
    highest = lax.Precision.HIGHEST

    def one_block(block_number):
        start = (block_number * BLK).astype(jnp.int32)
        own_block = lax.dynamic_slice_in_dim(values, start, BLK, 0)
        own_inverse = lax.dynamic_slice_in_dim(inverse_norm, start, BLK, 0)
        window_blocks = (block_number + jnp.arange(WINDOW, dtype=jnp.int32)) % block_count
        col_ids = (window_blocks[:, None] * BLK + jnp.arange(BLK, dtype=jnp.int32)[None, :]).reshape(-1)
        col_ids = col_ids.astype(jnp.int32)
        partner = jnp.take(values, col_ids, axis=0)
        partner_swapped = jnp.take(swapped, col_ids, axis=0)
        partner_inverse = jnp.take(inverse_norm, col_ids, axis=0)
        direct = jnp.einsum('irc,jrc->ijc', own_block, partner, precision=highest)
        mixed_terms = jnp.einsum('irc,jrc->ijc', own_block, partner_swapped, precision=highest)
        real_part = direct[:, :, :half_width] + direct[:, :, half_width:]
        imag_part = mixed_terms[:, :, half_width:] - mixed_terms[:, :, :half_width]
        cross_spectrum = jnp.concatenate([real_part, imag_part], axis=2)
        correlation = jnp.einsum('ijq,qs->ijs', cross_spectrum, forward, precision=highest)
        cosine = correlation * own_inverse[:, None, None] * partner_inverse[None, :, None]
        row_ids = start + jnp.arange(BLK, dtype=jnp.int32)
        keep_mask = jnp.where(row_ids[:, None] == col_ids[None, :], 0.0, 1.0).astype(jnp.float32)
        weights = jnp.exp(concentration * cosine) * keep_mask[:, :, None]
        spectral = jnp.einsum('ijs,sq->ijq', weights, backward, precision=highest)
        degree = lax.optimization_barrier(jnp.sum(spectral[:, :, 0], axis=1))
        rounded = spectral.astype(jnp.bfloat16).astype(jnp.float32)
        weight_real = jnp.concatenate([rounded[:, :, :half_width], rounded[:, :, :half_width]], axis=2)
        weight_imag = jnp.concatenate([-rounded[:, :, half_width:], rounded[:, :, half_width:]], axis=2)
        filtered = jnp.einsum('ijc,jrc->irc', weight_real, partner, precision=highest)
        filtered = filtered + jnp.einsum('ijc,jrc->irc', weight_imag, partner_swapped, precision=highest)
        return (filtered, degree)
    filtered, degree = lax.map(one_block, block_numbers)
    filtered = filtered.reshape(NIMG, R, A)
    degree = degree.reshape(NIMG)
    smoothed = filtered / degree[:, None, None]
    return (smoothed, jnp.log(degree))
```

```python
import functools
import math

import jax
import jax.numpy as jnp
import numpy as np
from jax import lax
from jax.experimental import pallas as pl
from jax.experimental.pallas import tpu as pltpu
from jax.sharding import PartitionSpec as P

epsilon = 1e-06
concentration = 40.0


def angle_tables(angular):
    half = angular // 2
    product = np.outer(np.arange(half), np.arange(angular)) % angular
    phase = product.astype(np.float32) * np.float32(2.0 * math.pi / angular)
    real, imag = np.cos(phase), -np.sin(phase)
    forward = np.concatenate([real, real, imag, -imag], axis=0)
    backward = np.concatenate([real, real, imag, -imag], axis=0).T
    return forward.astype(np.float32), np.ascontiguousarray(backward).astype(np.float32)


def is_power_of_two(n):
    return n & (n - 1) == 0


def moved(array, axis, pairs):
    return lax.ppermute(array, axis, pairs)


def flipped(array, axis, by):
    return moved(array, axis, [(i, i ^ by) for i in range(lax.axis_size(axis))])


def shifted(array, axis, by):
    count = lax.axis_size(axis)
    return moved(array, axis, [(i, (i + by) % count) for i in range(count)])


def slice_owner(position, step, count):
    if is_power_of_two(count):
        return position ^ step
    return (position + step) % count


def radial_slices(local):
    count = lax.axis_size("off")
    if is_power_of_two(count):
        return [local] + [flipped(local, "off", k) for k in range(1, count)]
    return [local] + [shifted(local, "off", -k) for k in range(1, count)]


def assemble_kernel(*refs):
    *slices, out, wide = refs
    images, depth, angular = slices[0].shape
    for k, piece in enumerate(slices):
        wide[...] = piece[...].astype(jnp.float32).reshape(images * depth, angular)
        for r in range(depth):
            rows = wide[pl.ds(r, images, stride=depth), :]
            out[k * depth + r] = rows.astype(out.dtype)


def assemble(slices):
    images, depth, angular = slices[0].shape
    vmem = pl.BlockSpec(memory_space=pltpu.VMEM)
    return pl.pallas_call(
        assemble_kernel,
        out_shape=jax.ShapeDtypeStruct((len(slices) * depth, images, angular), slices[0].dtype),
        in_specs=[vmem] * len(slices),
        out_specs=vmem,
        scratch_shapes=[pltpu.VMEM((images * depth, angular), jnp.float32)],
        name="assemble",
    )(*slices)


def window_blocks(column):
    count = lax.axis_size("blk")
    ranges = lax.axis_size("off")
    window = ranges * min(8, count // ranges)
    if window == count and is_power_of_two(count):
        groups = [column]
        bits = [1 << b for b in range(1, count.bit_length() - 1)]
        while bits:
            pair, bits = bits[:2], bits[2:]
            flips = [pair[0]] if len(pair) == 1 else [pair[0], pair[1], pair[0] | pair[1]]
            groups = groups + [flipped(g, "blk", f) for f in flips for g in groups]
        if count > 1:
            groups = groups + [flipped(g, "blk", 1) for g in groups]
        return [g[None] for g in groups]
    group = column[None]
    while group.shape[0] < window:
        held = group.shape[0]
        group = jnp.concatenate(
            [group, shifted(group[: min(held, window - held)], "blk", -held)], axis=0
        )
    return [group]


def filter_kernel(ranges, forward, backward, *refs):
    *groups, out, log_degree, own, direct_own, swapped_own, terms, norms, real_w, imag_w = refs
    _, radial, images, angular = groups[0].shape
    half = angular // 2
    rows = images // ranges
    depth = radial // ranges
    place = lax.axis_index("off")
    first = place * rows
    f32 = jnp.float32
    blocks = sum(g.shape[0] for g in groups)
    partners = blocks * images

    def spread(r, carry):
        own[...] = groups[0][0, r].astype(f32)
        for i in range(rows):
            row = own[pl.ds(first + i, 1), :]
            direct_own[i, r] = jnp.broadcast_to(row, (8, angular))
            swapped_own[i, r] = jnp.broadcast_to(pltpu.roll(row, half, 1), (8, angular))
        return carry

    lax.fori_loop(0, radial, spread, 0)

    def cross(group, b, start):
        def step(r, carry):
            direct, mixed, square = carry
            direct, mixed = list(direct), list(mixed)
            x = group[b, r].astype(f32).reshape(images // 8, 8, angular)
            for i in range(rows):
                direct[i] = direct[i] + direct_own[i, r][None] * x
                mixed[i] = mixed[i] + swapped_own[i, r][None] * x
            return tuple(direct), tuple(mixed), square + x * x

        zero = jnp.zeros((images // 8, 8, angular), f32)
        direct, mixed, square = lax.fori_loop(
            0, radial, step, ((zero,) * rows, (zero,) * rows, zero), unroll=4
        )
        for i in range(rows):
            at = pl.ds(i * partners + start, images)
            terms[at, :angular] = direct[i].reshape(images, angular)
            terms[at, angular:] = mixed[i].reshape(images, angular)
        norms[pl.ds(start, images), :] = square.reshape(images, angular)

    start = 0
    for group in groups:
        count = group.shape[0]
        if count == 1:
            cross(group, 0, start)
        else:

            def one(b, carry, group=group, start=start):
                cross(group, b, pl.multiple_of(start + b * images, images))
                return carry

            lax.fori_loop(0, count, one, 0)
        start += count * images

    highest = lax.Precision.HIGHEST
    correlation = jnp.dot(terms[...], forward[...], precision=highest, preferred_element_type=f32)
    inverse = lax.rsqrt(jnp.sum(norms[...], axis=1, keepdims=True) + epsilon)
    numbers = lax.broadcasted_iota(jnp.int32, (partners, angular), 0)
    weights = []
    for i in range(rows):
        mine = direct_own[i, :, 0, :]
        own_inverse = lax.rsqrt(jnp.sum(mine * mine, keepdims=True) + epsilon)
        cosine = correlation[i * partners : (i + 1) * partners] * own_inverse * inverse
        weights.append(jnp.where(numbers == first + i, 0.0, jnp.exp(concentration * cosine)))
    spectral = jnp.dot(
        jnp.concatenate(weights, axis=0), backward[...], precision=highest, preferred_element_type=f32
    )
    scales = []
    logs = []
    for i in range(rows):
        part = spectral[i * partners : (i + 1) * partners]
        degree = jnp.sum(part[:, :angular], axis=0, keepdims=True)[:, :1]
        scales.append(1.0 / degree)
        logs.append(jnp.log(degree))
        real_w[i] = part[:, :angular].astype(jnp.bfloat16).astype(f32)
        imag_w[i] = part[:, angular:].astype(jnp.bfloat16).astype(f32)
    log_degree[...] = jnp.broadcast_to(jnp.concatenate(logs, axis=0), (rows, angular))

    def filtered(pair, carry):
        pair_rows = (2 * pair, 2 * pair + 1)
        zero = jnp.zeros((8, angular), f32)
        sums = ((zero,) * rows, (zero,) * rows), ((zero,) * rows, (zero,) * rows)

        def accumulate(group, b, start, sums):
            new = [(list(s[0]), list(s[1])) for s in sums]
            xs = [group[b, r].astype(f32) for r in pair_rows]
            for v in range(images // 8):
                for i in range(rows):
                    real = real_w[i, pl.ds(start + 8 * v, 8), :]
                    imag = imag_w[i, pl.ds(start + 8 * v, 8), :]
                    for n in range(2):
                        x = xs[n][8 * v : 8 * v + 8]
                        new[n][0][i] = new[n][0][i] + real * x
                        new[n][1][i] = new[n][1][i] + imag * x
            return tuple((tuple(a), tuple(b)) for a, b in new)

        start = 0
        for group in groups:
            count = group.shape[0]
            if count == 1:
                sums = accumulate(group, 0, start, sums)
            else:
                sums = lax.fori_loop(
                    0,
                    count,
                    lambda b, s, group=group, start=start: accumulate(
                        group, b, pl.multiple_of(start + b * images, images), s
                    ),
                    sums,
                )
            start += count * images
        for n in range(2):
            r = pair_rows[n]
            target = slice_owner(place, r // depth, ranges) * depth + r % depth
            for i in range(rows):
                real = jnp.sum(sums[n][0][i], axis=0, keepdims=True)
                imag = jnp.sum(sums[n][1][i], axis=0, keepdims=True)
                out[i, pl.ds(target, 1), :] = (real + pltpu.roll(imag, half, 1)) * scales[i]
        return carry

    lax.fori_loop(0, radial // 2, filtered, 0)


def filter_images(groups, ranges):
    _, radial, images, angular = groups[0].shape
    rows = images // ranges
    partners = images * sum(g.shape[0] for g in groups)
    forward, backward = angle_tables(angular)
    vmem = pl.BlockSpec(memory_space=pltpu.VMEM)
    f32 = jnp.float32
    return pl.pallas_call(
        functools.partial(filter_kernel, ranges),
        out_shape=(
            jax.ShapeDtypeStruct((rows, radial, angular), f32),
            jax.ShapeDtypeStruct((rows, angular), f32),
        ),
        in_specs=[vmem] * (2 + len(groups)),
        out_specs=(vmem, vmem),
        scratch_shapes=[
            pltpu.VMEM((images, angular), f32),
            pltpu.VMEM((rows, radial, 8, angular), f32),
            pltpu.VMEM((rows, radial, 8, angular), f32),
            pltpu.VMEM((rows * partners, 2 * angular), f32),
            pltpu.VMEM((partners, angular), f32),
            pltpu.VMEM((rows, partners, angular), f32),
            pltpu.VMEM((rows, partners, angular), f32),
        ],
        compiler_params=pltpu.CompilerParams(vmem_limit_bytes=48 * 1024 * 1024),
        name="filter",
    )(forward, backward, *groups)


def body(coefficients):
    ranges = lax.axis_size("off")
    column = assemble(radial_slices(coefficients))
    smoothed, log_degree = filter_images(window_blocks(column), ranges)
    return smoothed, log_degree[:, 0]


def solution(mesh):
    return jax.shard_map(
        body,
        mesh=mesh,
        in_specs=(P("blk", "off", None),),
        out_specs=(P(("blk", "off"), None, None), P(("blk", "off"))),
        check_vma=False,
    )
```

```python
import functools
import math

import jax
import jax.numpy as jnp
import numpy as np
from jax import lax
from jax.experimental import pallas as pl
from jax.experimental.pallas import tpu as pltpu
from jax.sharding import PartitionSpec as P

epsilon = 1e-06
concentration = 40.0


def split(array):
    high = array.astype(jnp.bfloat16)
    return high, (array - high.astype(jnp.float32)).astype(jnp.bfloat16)


def angle_tables(angular):
    half = angular // 2
    product = np.outer(np.arange(half), np.arange(angular)) % angular
    phase = product.astype(np.float32) * np.float32(2.0 * math.pi / angular)
    real, imag = np.cos(phase), -np.sin(phase)
    forward = np.concatenate([real, real, imag, -imag], axis=0).astype(np.float32)
    high = forward.astype(jnp.bfloat16)
    low = (forward - high.astype(np.float32)).astype(jnp.bfloat16)
    return (
        np.concatenate([high, low], axis=1),
        np.ascontiguousarray(np.concatenate([high.T, high.T], axis=0)),
        np.ascontiguousarray(low.T),
    )


def is_power_of_two(n):
    return n & (n - 1) == 0


def moved(array, axis, pairs):
    return lax.ppermute(array, axis, pairs)


def flipped(array, axis, by):
    return moved(array, axis, [(i, i ^ by) for i in range(lax.axis_size(axis))])


def shifted(array, axis, by):
    count = lax.axis_size(axis)
    return moved(array, axis, [(i, (i + by) % count) for i in range(count)])


def slice_owner(position, step, count):
    if is_power_of_two(count):
        return position ^ step
    return (position + step) % count


def vmem():
    return pl.BlockSpec(memory_space=pltpu.VMEM)


def small_kernel(kernel, outs, count, name, limit, scratch=(), cycles=1000):
    return pl.pallas_call(
        kernel,
        out_shape=outs,
        in_specs=[vmem()] * count,
        out_specs=jax.tree.map(lambda _: vmem(), outs),
        scratch_shapes=scratch,
        compiler_params=pltpu.CompilerParams(vmem_limit_bytes=limit),
        cost_estimate=pl.CostEstimate(flops=cycles * 1024, bytes_accessed=0, transcendentals=0),
        name=name,
    )


def radial_first(source, wide, out, start):
    images, depth, angular = source.shape
    wide[...] = source[...].astype(jnp.float32).reshape(images * depth, angular)
    for r in range(depth):
        out[start + r] = wide[pl.ds(r, images, stride=depth), :].astype(out.dtype)


def turn_kernel(source, out, wide):
    radial_first(source, wide, out, 0)


def assemble_kernel(*refs):
    *slices, own, out, wide = refs
    depth = own.shape[0]
    out[:depth] = own[...]
    for k, piece in enumerate(slices[::-1]):
        radial_first(piece, wide, out, (k + 1) * depth)


def own_column(local):
    images, depth, angular = local.shape
    count = lax.axis_size("off")
    wide = [pltpu.VMEM((images * depth, angular), jnp.float32)]
    slices = [
        flipped(local, "off", k) if is_power_of_two(count) else shifted(local, "off", -k)
        for k in range(count - 1, 0, -1)
    ]
    turned = jax.ShapeDtypeStruct((depth, images, angular), local.dtype)
    whole = jax.ShapeDtypeStruct((count * depth, images, angular), local.dtype)
    own = small_kernel(turn_kernel, turned, 1, "turn", 1 << 21, wide, 100)(local)
    return small_kernel(assemble_kernel, whole, count, "assemble", 1 << 21, wide, 100)(*slices, own)


def hold_kernel(array, token, out):
    out[...] = array[...]


def hold(array, token):
    return small_kernel(
        hold_kernel, jax.ShapeDtypeStruct(array.shape, array.dtype), 2, "hold", 1 << 21, (), 100
    )(array, token)


def filter_window(column, run):
    count = lax.axis_size("blk")
    ranges = lax.axis_size("off")
    window = ranges * min(8, count // ranges)
    if window == count and count > 2 and is_power_of_two(count):
        far = [flipped(column, "blk", flip) for flip in range(count - 2, 0, -2)]
        carry = run((), [column], False)
        blocks = [hold(block, carry[2]) for block in far]
        twin = flipped(column, "blk", 1)
        carry = run(carry, blocks + [twin], False)
        return run(carry, [flipped(block, "blk", 1) for block in blocks], True)
    group = column[None]
    while group.shape[0] < window:
        held = group.shape[0]
        group = jnp.concatenate(
            [group, shifted(group[: min(held, window - held)], "blk", -held)], axis=0
        )
    return run((), [group], True)


def spread_kernel(ranges, column, direct_own, swapped_own, own_inverse, wide):
    radial, images, angular = column.shape
    rows = images // ranges
    first = lax.axis_index("off") * rows

    def step(r, squares):
        wide[r] = column[r].astype(jnp.float32)
        new = []
        for i in range(rows):
            row = wide[r, pl.ds(first + i, 1), :]
            direct_own[i, r] = jnp.broadcast_to(row, (8, angular))
            swapped_own[i, r] = jnp.broadcast_to(pltpu.roll(row, angular // 2, 1), (8, angular))
            new.append(squares[i] + row * row)
        return tuple(new)

    zero = jnp.zeros((1, angular), jnp.float32)
    squares = lax.fori_loop(0, radial, step, (zero,) * rows, unroll=8)
    for i in range(rows):
        total = jnp.sum(squares[i], axis=1, keepdims=True) + epsilon
        own_inverse[i : i + 1, :] = jnp.broadcast_to(lax.rsqrt(total), (1, angular))


def spread_own(column, ranges):
    radial, images, angular = column.shape
    rows = images // ranges
    tiles = jax.ShapeDtypeStruct((rows, radial, 8, angular), jnp.float32)
    return small_kernel(
        functools.partial(spread_kernel, ranges),
        (tiles, tiles, jax.ShapeDtypeStruct((rows, angular), jnp.float32)),
        1,
        "spread",
        1 << 22,
        [pltpu.VMEM((radial, images, angular), jnp.float32)],
        1000,
    )(column)


def fold(tiles):
    rows = tiles[0].shape[0]
    number = lax.broadcasted_iota(jnp.int32, tiles[0].shape, 0)
    step = 1
    while step < rows:
        low = (number // step) % 2 == 0
        tiles = [
            jnp.where(low, a, b) + pltpu.roll(jnp.where(low, b, a), step, 0)
            for a, b in zip(tiles[::2], tiles[1::2])
        ]
        step *= 2
    return tiles[0]


def filter_kernel(ranges, count, is_first, is_last, *refs):
    forward, backward, backward_low, direct_own, swapped_own, own_inverse, *refs = refs
    groups, refs = refs[:count], refs[count:]
    if not is_first:
        real_before, imag_before, degree_before, *refs = refs
    if is_last:
        out, log_degree, real_sum, imag_sum, *refs = refs
    else:
        real_sum, imag_sum, degrees, *refs = refs
    terms, norms, real_w, imag_w = refs
    _, radial, images, angular = groups[0].shape
    half = angular // 2
    rows = images // ranges
    depth = radial // ranges
    place = lax.axis_index("off")
    f32 = jnp.float32
    partners = images * sum(g.shape[0] for g in groups)

    def each_block(do, carry):
        start = 0
        for group in groups:
            blocks = group.shape[0]
            if blocks == 1:
                carry = do(group, 0, start, carry)
            else:

                def one(b, c, group=group, start=start):
                    return do(group, b, pl.multiple_of(start + b * images, images), c)

                carry = lax.fori_loop(0, blocks, one, carry)
            start += blocks * images
        return carry

    def cross(group, b, start, carry):
        def step(r, sums):
            direct, mixed, square = sums
            x = group[b, r].astype(f32).reshape(images // 8, 8, angular)
            direct = tuple(direct[i] + direct_own[i, r][None] * x for i in range(rows))
            mixed = tuple(mixed[i] + swapped_own[i, r][None] * x for i in range(rows))
            return direct, mixed, square + x * x

        zero = jnp.zeros((images // 8, 8, angular), f32)
        direct, mixed, square = lax.fori_loop(
            0, radial, step, ((zero,) * rows, (zero,) * rows, zero), unroll=True
        )
        for i in range(rows):
            at = pl.ds(i * partners + start, images)
            terms[at, :angular] = direct[i].reshape(images, angular)
            terms[at, angular:] = mixed[i].reshape(images, angular)
        norms[pl.ds(start, images), :] = square.reshape(images, angular)
        return carry

    each_block(cross, 0)

    high, low = split(terms[...])
    both = jnp.dot(high, forward[...], preferred_element_type=f32)
    rest = jnp.dot(low, forward[:, :angular], preferred_element_type=f32)
    correlation = both[:, :angular] + (both[:, angular:] + rest)
    inverse = lax.rsqrt(jnp.sum(norms[...], axis=1, keepdims=True) + epsilon) * concentration
    weights = []
    for i in range(rows):
        exponent = correlation[i * partners : (i + 1) * partners] * own_inverse[i : i + 1] * inverse
        weight = jnp.exp(exponent)
        if is_first:
            numbers = lax.broadcasted_iota(jnp.int32, (partners, angular), 0)
            weight = jnp.where(numbers == place * rows + i, 0.0, weight)
        weights.append(weight)
    high, low = split(jnp.concatenate(weights, axis=0))
    spectral = jnp.dot(jnp.concatenate([high, low], axis=1), backward[...], preferred_element_type=f32)
    spectral = spectral + jnp.dot(high, backward_low[...], preferred_element_type=f32)
    scales = []
    for i in range(rows):
        part = spectral[i * partners : (i + 1) * partners]
        degree = jnp.sum(part[:, :angular], axis=0, keepdims=True)
        if not is_first:
            degree = degree + degree_before[i : i + 1]
        if is_last:
            scales.append(1.0 / degree[:, :1])
            log_degree[i] = jnp.log(degree)[0, 0]
        else:
            degrees[i : i + 1, :] = degree
        real_w[i] = part[:, :angular].astype(jnp.bfloat16).astype(f32)
        imag_w[i] = part[:, angular:].astype(jnp.bfloat16).astype(f32)

    def filtered(pair, carry):
        places = (2 * pair, 2 * pair + 1)
        if is_first:
            zero = jnp.zeros((8, angular), f32)
            start_sums = (((zero,) * rows, (zero,) * rows),) * 2
        else:
            start_sums = tuple(
                (
                    tuple(real_before[i, r] for i in range(rows)),
                    tuple(imag_before[i, r] for i in range(rows)),
                )
                for r in places
            )

        def accumulate(group, b, start, sums):
            new = [(list(s[0]), list(s[1])) for s in sums]
            xs = [group[b, r].astype(f32) for r in places]
            for v in range(images // 8):
                for i in range(rows):
                    real = real_w[i, pl.ds(start + 8 * v, 8), :]
                    imag = imag_w[i, pl.ds(start + 8 * v, 8), :]
                    for n in range(2):
                        x = xs[n][8 * v : 8 * v + 8]
                        new[n][0][i] = new[n][0][i] + real * x
                        new[n][1][i] = new[n][1][i] + imag * x
            return tuple((tuple(a), tuple(b)) for a, b in new)

        totals = each_block(accumulate, start_sums)
        for n in range(2):
            for i in range(rows):
                real_sum[i, places[n]] = totals[n][0][i]
                imag_sum[i, places[n]] = totals[n][1][i]
        return carry

    lax.fori_loop(0, radial // 2, filtered, 0, unroll=2)

    if is_last:
        for k in range(ranges):
            for part in range(depth // 8):
                at = k * depth + 8 * part
                target = slice_owner(place, k, ranges) * depth + 8 * part
                for i in range(rows):
                    real = fold([real_sum[i, at + n] for n in range(8)])
                    imag = fold([imag_sum[i, at + n] for n in range(8)])
                    total = real + pltpu.roll(imag, half, 1)
                    out[i, pl.ds(pl.multiple_of(target, 8), 8), :] = total * scales[i]


def filter_stage(ranges, own, tables, carry, groups, is_last):
    groups = [g.reshape(-1, *g.shape[-3:]) for g in groups]
    _, radial, images, angular = groups[0].shape
    rows = images // ranges
    f32 = jnp.float32
    sums = jax.ShapeDtypeStruct((rows, radial, 8, angular), f32)
    partners = images * sum(g.shape[0] for g in groups)
    scratch = [
        pltpu.VMEM((rows * partners, 2 * angular), f32),
        pltpu.VMEM((partners, angular), f32),
        pltpu.VMEM((rows, partners, angular), f32),
        pltpu.VMEM((rows, partners, angular), f32),
    ]
    if is_last:
        outs = (
            jax.ShapeDtypeStruct((rows, radial, angular), f32),
            jax.ShapeDtypeStruct((rows,), f32),
        )
        out_specs = (vmem(), pl.BlockSpec(memory_space=pltpu.SMEM))
        scratch = [pltpu.VMEM(sums.shape, f32)] * 2 + scratch
    else:
        outs = (sums, sums, jax.ShapeDtypeStruct((rows, angular), f32))
        out_specs = (vmem(),) * 3
    operands = (*tables, *own, *groups, *carry)
    return pl.pallas_call(
        functools.partial(filter_kernel, ranges, len(groups), not carry, is_last),
        out_shape=outs,
        in_specs=[vmem()] * len(operands),
        out_specs=out_specs,
        scratch_shapes=scratch,
        compiler_params=pltpu.CompilerParams(
            vmem_limit_bytes=(40 if partners > 8 * images else 8) << 20
        ),
        cost_estimate=pl.CostEstimate(
            flops=4 * partners * radial * 1024 * rows, bytes_accessed=0, transcendentals=0
        ),
        name="filter",
    )(*operands)


def body(coefficients):
    ranges = lax.axis_size("off")
    column = own_column(coefficients)
    own = spread_own(column, ranges)
    tables = angle_tables(coefficients.shape[2])
    return filter_window(column, functools.partial(filter_stage, ranges, own, tables))


def solution(mesh):
    return jax.shard_map(
        body,
        mesh=mesh,
        in_specs=(P("blk", "off", None),),
        out_specs=(P(("blk", "off"), None, None), P(("blk", "off"))),
        check_vma=False,
    )
```

```python
import functools
import math

import jax
import jax.numpy as jnp
import numpy as np
from jax import lax
from jax.experimental import pallas as pl
from jax.experimental.pallas import tpu as pltpu
from jax.sharding import PartitionSpec as P

epsilon = 1e-06
concentration = 40.0


def split(array):
    high = array.astype(jnp.bfloat16)
    return high, (array - high.astype(jnp.float32)).astype(jnp.bfloat16)


def angle_tables(angular):
    half = angular // 2
    product = np.outer(np.arange(half), np.arange(angular)) % angular
    phase = product.astype(np.float32) * np.float32(2.0 * math.pi / angular)
    real, imag = np.cos(phase), -np.sin(phase)
    forward = np.concatenate([real, real, imag, -imag], axis=0).astype(np.float32)
    high = forward.astype(jnp.bfloat16)
    low = (forward - high.astype(np.float32)).astype(jnp.bfloat16)
    return (
        np.concatenate([high, low], axis=1),
        np.ascontiguousarray(np.concatenate([high.T, high.T], axis=0)),
        np.ascontiguousarray(low.T),
    )


def is_power_of_two(n):
    return n & (n - 1) == 0


def moved(array, axis, pairs):
    return lax.ppermute(array, axis, pairs)


def flipped(array, axis, by):
    return moved(array, axis, [(i, i ^ by) for i in range(lax.axis_size(axis))])


def shifted(array, axis, by):
    count = lax.axis_size(axis)
    return moved(array, axis, [(i, (i + by) % count) for i in range(count)])


def vmem():
    return pl.BlockSpec(memory_space=pltpu.VMEM)


def small_kernel(kernel, outs, count, name, limit, scratch=(), cycles=1000):
    return pl.pallas_call(
        kernel,
        out_shape=outs,
        in_specs=[vmem()] * count,
        out_specs=jax.tree.map(lambda _: vmem(), outs),
        scratch_shapes=scratch,
        compiler_params=pltpu.CompilerParams(vmem_limit_bytes=limit),
        cost_estimate=pl.CostEstimate(flops=cycles * 1024, bytes_accessed=0, transcendentals=0),
        name=name,
    )


def radial_first(source, wide, out, start):
    images, depth, angular = source.shape
    wide[...] = source[...].astype(jnp.float32).reshape(images * depth, angular)
    for r in range(depth):
        out[start + r] = wide[pl.ds(r, images, stride=depth), :].astype(out.dtype)


def spread_kernel(ranges, column, direct_own, swapped_own, own_inverse, wide):
    radial, images, angular = column.shape
    rows = images // ranges
    first = lax.axis_index("off") * rows

    def step(r, squares):
        wide[r] = column[r].astype(jnp.float32)
        new = []
        for i in range(rows):
            row = wide[r, pl.ds(first + i, 1), :]
            direct_own[i, r] = jnp.broadcast_to(row, (8, angular))
            swapped_own[i, r] = jnp.broadcast_to(pltpu.roll(row, angular // 2, 1), (8, angular))
            new.append(squares[i] + row * row)
        return tuple(new)

    zero = jnp.zeros((1, angular), jnp.float32)
    squares = lax.fori_loop(0, radial, step, (zero,) * rows, unroll=8)
    for i in range(rows):
        total = jnp.sum(squares[i], axis=1, keepdims=True) + epsilon
        own_inverse[i : i + 1, :] = jnp.broadcast_to(lax.rsqrt(total), (1, angular))


def spread_own(column, ranges):
    radial, images, angular = column.shape
    rows = images // ranges
    tiles = jax.ShapeDtypeStruct((rows, radial, 8, angular), jnp.float32)
    return small_kernel(
        functools.partial(spread_kernel, ranges),
        (tiles, tiles, jax.ShapeDtypeStruct((rows, angular), jnp.float32)),
        1,
        "spread",
        1 << 22,
        [pltpu.VMEM((radial, images, angular), jnp.float32)],
        1000,
    )(column)


def fold(tiles):
    rows = tiles[0].shape[0]
    number = lax.broadcasted_iota(jnp.int32, tiles[0].shape, 0)
    step = 1
    while step < rows:
        low = (number // step) % 2 == 0
        tiles = [
            jnp.where(low, a, b) + pltpu.roll(jnp.where(low, b, a), step, 0)
            for a, b in zip(tiles[::2], tiles[1::2])
        ]
        step *= 2
    return tiles[0]


def filter_kernel(ranges, slice_place, count, is_first, is_last, *refs):
    forward, backward, backward_low, direct_own, swapped_own, own_inverse, *refs = refs
    groups, refs = refs[:count], refs[count:]
    if not is_first:
        real_before, imag_before, degree_before, *refs = refs
    if is_last:
        out, log_degree, real_sum, imag_sum, *refs = refs
    else:
        real_sum, imag_sum, degrees, *refs = refs
    terms, norms, real_w, imag_w = refs
    _, radial, images, angular = groups[0].shape
    half = angular // 2
    rows = images // ranges
    depth = radial // ranges
    place = lax.axis_index("off")
    f32 = jnp.float32
    partners = images * sum(g.shape[0] for g in groups)

    def each_block(do, carry):
        start = 0
        for group in groups:
            blocks = group.shape[0]
            if blocks == 1:
                carry = do(group, 0, start, carry)
            else:

                def one(b, c, group=group, start=start):
                    return do(group, b, pl.multiple_of(start + b * images, images), c)

                carry = lax.fori_loop(0, blocks, one, carry)
            start += blocks * images
        return carry

    def cross(group, b, start, carry):
        def step(r, sums):
            direct, mixed, square = sums
            x = group[b, r].astype(f32).reshape(images // 8, 8, angular)
            direct = tuple(direct[i] + direct_own[i, r][None] * x for i in range(rows))
            mixed = tuple(mixed[i] + swapped_own[i, r][None] * x for i in range(rows))
            return direct, mixed, square + x * x

        zero = jnp.zeros((images // 8, 8, angular), f32)
        direct, mixed, square = lax.fori_loop(
            0, radial, step, ((zero,) * rows, (zero,) * rows, zero), unroll=True
        )
        for i in range(rows):
            at = pl.ds(i * partners + start, images)
            terms[at, :angular] = direct[i].reshape(images, angular)
            terms[at, angular:] = mixed[i].reshape(images, angular)
        norms[pl.ds(start, images), :] = square.reshape(images, angular)
        return carry

    each_block(cross, 0)

    high, low = split(terms[...])
    both = jnp.dot(high, forward[...], preferred_element_type=f32)
    rest = jnp.dot(low, forward[:, :angular], preferred_element_type=f32)
    correlation = both[:, :angular] + (both[:, angular:] + rest)
    inverse = lax.rsqrt(jnp.sum(norms[...], axis=1, keepdims=True) + epsilon) * concentration
    weights = []
    for i in range(rows):
        exponent = correlation[i * partners : (i + 1) * partners] * own_inverse[i : i + 1] * inverse
        weight = jnp.exp(exponent)
        if is_first:
            numbers = lax.broadcasted_iota(jnp.int32, (partners, angular), 0)
            weight = jnp.where(numbers == place * rows + i, 0.0, weight)
        weights.append(weight)
    high, low = split(jnp.concatenate(weights, axis=0))
    spectral = jnp.dot(jnp.concatenate([high, low], axis=1), backward[...], preferred_element_type=f32)
    spectral = spectral + jnp.dot(high, backward_low[...], preferred_element_type=f32)
    scales = []
    for i in range(rows):
        part = spectral[i * partners : (i + 1) * partners]
        degree = jnp.sum(part[:, :angular], axis=0, keepdims=True)
        if not is_first:
            degree = degree + degree_before[i : i + 1]
        if is_last:
            scales.append(1.0 / degree[:, :1])
            log_degree[i] = jnp.log(degree)[0, 0]
        else:
            degrees[i : i + 1, :] = degree
        real_w[i] = part[:, :angular].astype(jnp.bfloat16).astype(f32)
        imag_w[i] = part[:, angular:].astype(jnp.bfloat16).astype(f32)

    def filtered(pair, carry):
        places = (2 * pair, 2 * pair + 1)
        if is_first:
            zero = jnp.zeros((8, angular), f32)
            start_sums = (((zero,) * rows, (zero,) * rows),) * 2
        else:
            start_sums = tuple(
                (
                    tuple(real_before[i, r] for i in range(rows)),
                    tuple(imag_before[i, r] for i in range(rows)),
                )
                for r in places
            )

        def accumulate(group, b, start, sums):
            new = [(list(s[0]), list(s[1])) for s in sums]
            xs = [group[b, r].astype(f32) for r in places]
            for v in range(images // 8):
                for i in range(rows):
                    real = real_w[i, pl.ds(start + 8 * v, 8), :]
                    imag = imag_w[i, pl.ds(start + 8 * v, 8), :]
                    for n in range(2):
                        x = xs[n][8 * v : 8 * v + 8]
                        new[n][0][i] = new[n][0][i] + real * x
                        new[n][1][i] = new[n][1][i] + imag * x
            return tuple((tuple(a), tuple(b)) for a, b in new)

        totals = each_block(accumulate, start_sums)
        for n in range(2):
            for i in range(rows):
                real_sum[i, places[n]] = totals[n][0][i]
                imag_sum[i, places[n]] = totals[n][1][i]
        return carry

    lax.fori_loop(0, radial // 2, filtered, 0, unroll=2)

    if is_last:
        for k in range(ranges):
            for part in range(depth // 8):
                at = k * depth + 8 * part
                target = slice_place(place, k) * depth + 8 * part
                for i in range(rows):
                    real = fold([real_sum[i, at + n] for n in range(8)])
                    imag = fold([imag_sum[i, at + n] for n in range(8)])
                    total = real + pltpu.roll(imag, half, 1)
                    out[i, pl.ds(pl.multiple_of(target, 8), 8), :] = total * scales[i]


def filter_stage(tables, slice_place, own, carry, groups, is_last):
    ranges = lax.axis_size("off")
    groups = [g.reshape(-1, *g.shape[-3:]) for g in groups]
    _, radial, images, angular = groups[0].shape
    rows = images // ranges
    f32 = jnp.float32
    sums = jax.ShapeDtypeStruct((rows, radial, 8, angular), f32)
    partners = images * sum(g.shape[0] for g in groups)
    scratch = [
        pltpu.VMEM((rows * partners, 2 * angular), f32),
        pltpu.VMEM((partners, angular), f32),
        pltpu.VMEM((rows, partners, angular), f32),
        pltpu.VMEM((rows, partners, angular), f32),
    ]
    if is_last:
        outs = (
            jax.ShapeDtypeStruct((rows, radial, angular), f32),
            jax.ShapeDtypeStruct((rows,), f32),
        )
        out_specs = (vmem(), pl.BlockSpec(memory_space=pltpu.SMEM))
        scratch = [pltpu.VMEM(sums.shape, f32)] * 2 + scratch
    else:
        outs = (sums, sums, jax.ShapeDtypeStruct((rows, angular), f32))
        out_specs = (vmem(),) * 3
    operands = (*tables, *own, *groups, *carry)
    return pl.pallas_call(
        functools.partial(filter_kernel, ranges, slice_place, len(groups), not carry, is_last),
        out_shape=outs,
        in_specs=[vmem()] * len(operands),
        out_specs=out_specs,
        scratch_shapes=scratch,
        compiler_params=pltpu.CompilerParams(
            vmem_limit_bytes=(40 if partners > 8 * images else 8) << 20
        ),
        cost_estimate=pl.CostEstimate(
            flops=4 * partners * radial * 1024 * rows, bytes_accessed=0, transcendentals=0
        ),
        name="filter",
    )(*operands)


def assemble_kernel(*refs):
    *slices, out, wide = refs
    depth = slices[0].shape[1]
    for k, piece in enumerate(slices[::-1]):
        radial_first(piece, wide, out, k * depth)


def assemble(slices):
    images, depth, angular = slices[0].shape
    whole = jax.ShapeDtypeStruct((len(slices) * depth, images, angular), slices[0].dtype)
    wide = [pltpu.VMEM((images * depth, angular), jnp.float32)]
    return small_kernel(assemble_kernel, whole, len(slices), "assemble", 1 << 21, wide, 100)(*slices)


def join_kernel(first, rest, token, out):
    depth = first.shape[0]
    out[:depth] = first[...]
    out[depth:] = rest[...]


def join(first, rest, token):
    depth, images, angular = rest.shape
    whole = jax.ShapeDtypeStruct((first.shape[0] + depth, images, angular), rest.dtype)
    return small_kernel(join_kernel, whole, 3, "join", 1 << 21, (), 100)(first, rest, token)


def by_flips(local, run):
    depth = local.shape[1]
    far = range(lax.axis_size("blk") - 2, 0, -2)
    slices = [flipped(local, "off", k) for k in range(lax.axis_size("off") - 1, 0, -1)]
    heads = assemble([flipped(local, "blk", flip) for flip in far][::-1] + [local])
    head = [heads[n * depth : (n + 1) * depth] for n in range(len(far) + 1)]
    rest = assemble(slices)
    rests = [flipped(rest, "blk", flip) for flip in far]
    column = join(head[0], rest, heads)
    run = functools.partial(run, spread_own(column, lax.axis_size("off")))
    carry = run((), [column], False)
    first = join(head[1], rests[0], carry[2])
    carry = run(carry, [first], False)
    others = [join(h, r, carry[2]) for h, r in zip(head[2:], rests[1:])]
    twins = [flipped(block, "blk", 1) for block in [column, first] + others]
    carry = run(carry, others + twins[:2], not others)
    return run(carry, twins[2:], True) if others else carry


def by_shifts(local, window, run):
    ranges = lax.axis_size("off")
    column = assemble([shifted(local, "off", -k) for k in range(ranges - 1, 0, -1)] + [local])
    group = column[None]
    while group.shape[0] < window:
        held = group.shape[0]
        more = shifted(group[: min(held, window - held)], "blk", -held)
        group = jnp.concatenate([group, more], axis=0)
    return run(spread_own(column, ranges), (), [group], True)


def body(coefficients):
    count, ranges = lax.axis_size("blk"), lax.axis_size("off")
    window = ranges * min(8, count // ranges)
    tables = angle_tables(coefficients.shape[2])
    flips = window == count and count > 2 and ranges > 1
    if flips and is_power_of_two(count) and is_power_of_two(ranges):
        stage = functools.partial(filter_stage, tables, lambda place, k: place ^ k)
        return by_flips(coefficients, stage)
    stage = functools.partial(filter_stage, tables, lambda place, k: (place + k) % ranges)
    return by_shifts(coefficients, window, stage)


def solution(mesh):
    return jax.shard_map(
        body,
        mesh=mesh,
        in_specs=(P("blk", "off", None),),
        out_specs=(P(("blk", "off"), None, None), P(("blk", "off"))),
        check_vma=False,
    )
```

```python
import functools
import math

import jax
import jax.numpy as jnp
import numpy as np
from jax import lax
from jax.experimental import pallas as pl
from jax.experimental.pallas import tpu as pltpu
from jax.sharding import PartitionSpec as P

epsilon = 1e-06
concentration = 40.0


def split(array):
    high = array.astype(jnp.bfloat16)
    return high, (array - high.astype(jnp.float32)).astype(jnp.bfloat16)


def angle_tables(angular):
    half = angular // 2
    product = np.outer(np.arange(half), np.arange(angular)) % angular
    phase = product.astype(np.float32) * np.float32(2.0 * math.pi / angular)
    real, imag = np.cos(phase), -np.sin(phase)
    forward = np.concatenate([real, real, imag, -imag], axis=0).astype(np.float32)
    high = forward.astype(jnp.bfloat16)
    low = (forward - high.astype(np.float32)).astype(jnp.bfloat16)
    return (
        np.concatenate([high, low], axis=1),
        np.ascontiguousarray(np.concatenate([high.T, high.T], axis=0)),
        np.ascontiguousarray(low.T),
    )


def is_power_of_two(n):
    return n & (n - 1) == 0


def moved(array, axis, pairs):
    return lax.ppermute(array, axis, pairs)


def flipped(array, axis, by):
    return moved(array, axis, [(i, i ^ by) for i in range(lax.axis_size(axis))])


def shifted(array, axis, by):
    count = lax.axis_size(axis)
    return moved(array, axis, [(i, (i + by) % count) for i in range(count)])


def vmem():
    return pl.BlockSpec(memory_space=pltpu.VMEM)


def small_kernel(kernel, outs, count, name, limit, scratch=(), cycles=1000):
    return pl.pallas_call(
        kernel,
        out_shape=outs,
        in_specs=[vmem()] * count,
        out_specs=jax.tree.map(lambda _: vmem(), outs),
        scratch_shapes=scratch,
        compiler_params=pltpu.CompilerParams(vmem_limit_bytes=limit),
        cost_estimate=pl.CostEstimate(flops=cycles * 1024, bytes_accessed=0, transcendentals=0),
        name=name,
    )


def radial_first(source, wide, out, start):
    images, depth, angular = source.shape
    wide[...] = source[...].astype(jnp.float32).reshape(images * depth, angular)
    for r in range(depth):
        out[start + r] = wide[pl.ds(r, images, stride=depth), :].astype(out.dtype)


def spread_kernel(ranges, column, direct_own, swapped_own, own_inverse, wide):
    radial, images, angular = column.shape
    rows = images // ranges
    first = lax.axis_index("off") * rows

    def step(r, squares):
        wide[r] = column[r].astype(jnp.float32)
        new = []
        for i in range(rows):
            row = wide[r, pl.ds(first + i, 1), :]
            direct_own[i, r] = jnp.broadcast_to(row, (8, angular))
            swapped_own[i, r] = jnp.broadcast_to(pltpu.roll(row, angular // 2, 1), (8, angular))
            new.append(squares[i] + row * row)
        return tuple(new)

    zero = jnp.zeros((1, angular), jnp.float32)
    squares = lax.fori_loop(0, radial, step, (zero,) * rows, unroll=8)
    for i in range(rows):
        total = jnp.sum(squares[i], axis=1, keepdims=True) + epsilon
        own_inverse[i : i + 1, :] = jnp.broadcast_to(lax.rsqrt(total), (1, angular))


def spread_own(column, ranges):
    radial, images, angular = column.shape
    rows = images // ranges
    tiles = jax.ShapeDtypeStruct((rows, radial, 8, angular), jnp.float32)
    return small_kernel(
        functools.partial(spread_kernel, ranges),
        (tiles, tiles, jax.ShapeDtypeStruct((rows, angular), jnp.float32)),
        1,
        "spread",
        1 << 22,
        [pltpu.VMEM((radial, images, angular), jnp.float32)],
        1000,
    )(column)


def fold(tiles):
    rows = tiles[0].shape[0]
    number = lax.broadcasted_iota(jnp.int32, tiles[0].shape, 0)
    step = 1
    while step < rows:
        low = (number // step) % 2 == 0
        tiles = [
            jnp.where(low, a, b) + pltpu.roll(jnp.where(low, b, a), step, 0)
            for a, b in zip(tiles[::2], tiles[1::2])
        ]
        step *= 2
    return tiles[0]


def filter_kernel(ranges, slice_place, count, is_first, is_last, *refs):
    forward, backward, backward_low, direct_own, swapped_own, own_inverse, *refs = refs
    groups, refs = refs[:count], refs[count:]
    if not is_first:
        real_before, imag_before, degree_before, *refs = refs
    if is_last:
        out, log_degree, real_sum, imag_sum, *refs = refs
    else:
        real_sum, imag_sum, degrees, *refs = refs
    terms, norms, real_w, imag_w = refs
    _, radial, images, angular = groups[0].shape
    half = angular // 2
    rows = images // ranges
    depth = radial // ranges
    place = lax.axis_index("off")
    f32 = jnp.float32
    partners = images * sum(g.shape[0] for g in groups)

    def each_block(do, carry):
        start = 0
        for group in groups:
            blocks = group.shape[0]
            if blocks == 1:
                carry = do(group, 0, start, carry)
            else:

                def one(b, c, group=group, start=start):
                    return do(group, b, pl.multiple_of(start + b * images, images), c)

                carry = lax.fori_loop(0, blocks, one, carry)
            start += blocks * images
        return carry

    def cross(group, b, start, carry):
        def step(r, sums):
            direct, mixed, square = sums
            x = group[b, r].astype(f32).reshape(images // 8, 8, angular)
            direct = tuple(direct[i] + direct_own[i, r][None] * x for i in range(rows))
            mixed = tuple(mixed[i] + swapped_own[i, r][None] * x for i in range(rows))
            return direct, mixed, square + x * x

        zero = jnp.zeros((images // 8, 8, angular), f32)
        direct, mixed, square = lax.fori_loop(
            0, radial, step, ((zero,) * rows, (zero,) * rows, zero), unroll=True
        )
        for i in range(rows):
            at = pl.ds(i * partners + start, images)
            terms[at, :angular] = direct[i].reshape(images, angular)
            terms[at, angular:] = mixed[i].reshape(images, angular)
        norms[pl.ds(start, images), :] = square.reshape(images, angular)
        return carry

    each_block(cross, 0)

    high, low = split(terms[...])
    both = jnp.dot(high, forward[...], preferred_element_type=f32)
    rest = jnp.dot(low, forward[:, :angular], preferred_element_type=f32)
    correlation = both[:, :angular] + (both[:, angular:] + rest)
    inverse = lax.rsqrt(jnp.sum(norms[...], axis=1, keepdims=True) + epsilon) * concentration
    weights = []
    for i in range(rows):
        exponent = correlation[i * partners : (i + 1) * partners] * own_inverse[i : i + 1] * inverse
        weight = jnp.exp(exponent)
        if is_first:
            numbers = lax.broadcasted_iota(jnp.int32, (partners, angular), 0)
            weight = jnp.where(numbers == place * rows + i, 0.0, weight)
        weights.append(weight)
    high, low = split(jnp.concatenate(weights, axis=0))
    spectral = jnp.dot(jnp.concatenate([high, low], axis=1), backward[...], preferred_element_type=f32)
    spectral = spectral + jnp.dot(high, backward_low[...], preferred_element_type=f32)
    scales = []
    for i in range(rows):
        part = spectral[i * partners : (i + 1) * partners]
        degree = jnp.sum(part[:, :angular], axis=0, keepdims=True)
        if not is_first:
            degree = degree + degree_before[i : i + 1]
        if is_last:
            scales.append(1.0 / degree[:, :1])
            log_degree[i] = jnp.log(degree)[0, 0]
        else:
            degrees[i : i + 1, :] = degree
        real_w[i] = part[:, :angular].astype(jnp.bfloat16).astype(f32)
        imag_w[i] = part[:, angular:].astype(jnp.bfloat16).astype(f32)

    def filtered(pair, carry):
        places = (2 * pair, 2 * pair + 1)
        if is_first:
            zero = jnp.zeros((8, angular), f32)
            start_sums = (((zero,) * rows, (zero,) * rows),) * 2
        else:
            start_sums = tuple(
                (
                    tuple(real_before[i, r] for i in range(rows)),
                    tuple(imag_before[i, r] for i in range(rows)),
                )
                for r in places
            )

        def accumulate(group, b, start, sums):
            new = [(list(s[0]), list(s[1])) for s in sums]
            xs = [group[b, r].astype(f32) for r in places]
            for v in range(images // 8):
                for i in range(rows):
                    real = real_w[i, pl.ds(start + 8 * v, 8), :]
                    imag = imag_w[i, pl.ds(start + 8 * v, 8), :]
                    for n in range(2):
                        x = xs[n][8 * v : 8 * v + 8]
                        new[n][0][i] = new[n][0][i] + real * x
                        new[n][1][i] = new[n][1][i] + imag * x
            return tuple((tuple(a), tuple(b)) for a, b in new)

        totals = each_block(accumulate, start_sums)
        for n in range(2):
            for i in range(rows):
                real_sum[i, places[n]] = totals[n][0][i]
                imag_sum[i, places[n]] = totals[n][1][i]
        return carry

    lax.fori_loop(0, radial // 2, filtered, 0, unroll=True)

    if is_last:
        for k in range(ranges):
            for part in range(depth // 8):
                at = k * depth + 8 * part
                target = slice_place(place, k) * depth + 8 * part
                for i in range(rows):
                    real = fold([real_sum[i, at + n] for n in range(8)])
                    imag = fold([imag_sum[i, at + n] for n in range(8)])
                    total = real + pltpu.roll(imag, half, 1)
                    out[i, pl.ds(pl.multiple_of(target, 8), 8), :] = total * scales[i]


def filter_stage(tables, slice_place, own, carry, groups, is_last):
    ranges = lax.axis_size("off")
    groups = [g.reshape(-1, *g.shape[-3:]) for g in groups]
    _, radial, images, angular = groups[0].shape
    rows = images // ranges
    f32 = jnp.float32
    sums = jax.ShapeDtypeStruct((rows, radial, 8, angular), f32)
    partners = images * sum(g.shape[0] for g in groups)
    scratch = [
        pltpu.VMEM((rows * partners, 2 * angular), f32),
        pltpu.VMEM((partners, angular), f32),
        pltpu.VMEM((rows, partners, angular), f32),
        pltpu.VMEM((rows, partners, angular), f32),
    ]
    if is_last:
        outs = (
            jax.ShapeDtypeStruct((rows, radial, angular), f32),
            jax.ShapeDtypeStruct((rows,), f32),
        )
        out_specs = (vmem(), pl.BlockSpec(memory_space=pltpu.SMEM))
        scratch = [pltpu.VMEM(sums.shape, f32)] * 2 + scratch
    else:
        outs = (sums, sums, jax.ShapeDtypeStruct((rows, angular), f32))
        out_specs = (vmem(),) * 3
    operands = (*tables, *own, *groups, *carry)
    return pl.pallas_call(
        functools.partial(filter_kernel, ranges, slice_place, len(groups), not carry, is_last),
        out_shape=outs,
        in_specs=[vmem()] * len(operands),
        out_specs=out_specs,
        scratch_shapes=scratch,
        compiler_params=pltpu.CompilerParams(
            vmem_limit_bytes=(40 if partners > 8 * images else 8) << 20
        ),
        cost_estimate=pl.CostEstimate(
            flops=4 * partners * radial * 1024 * rows, bytes_accessed=0, transcendentals=0
        ),
        name="filter",
    )(*operands)


def assemble_kernel(*refs):
    *slices, out, wide = refs
    depth = slices[0].shape[1]
    for k, piece in enumerate(slices[::-1]):
        radial_first(piece, wide, out, k * depth)


def assemble(slices):
    images, depth, angular = slices[0].shape
    whole = jax.ShapeDtypeStruct((len(slices) * depth, images, angular), slices[0].dtype)
    wide = [pltpu.VMEM((images * depth, angular), jnp.float32)]
    return small_kernel(assemble_kernel, whole, len(slices), "assemble", 1 << 21, wide, 100)(*slices)


def join_kernel(first, rest, token, out):
    depth = first.shape[0]
    out[:depth] = first[...]
    out[depth:] = rest[...]


def join(first, rest, token):
    depth, images, angular = rest.shape
    whole = jax.ShapeDtypeStruct((first.shape[0] + depth, images, angular), rest.dtype)
    return small_kernel(join_kernel, whole, 3, "join", 1 << 21, (), 100)(first, rest, token)


def by_flips(local, run):
    depth = local.shape[1]
    far = range(lax.axis_size("blk") - 2, 0, -2)
    slices = [flipped(local, "off", k) for k in range(lax.axis_size("off") - 1, 0, -1)]
    heads = assemble([flipped(local, "blk", flip) for flip in far][::-1] + [local])
    head = [heads[n * depth : (n + 1) * depth] for n in range(len(far) + 1)]
    rest = assemble(slices)
    rests = [flipped(rest, "blk", flip) for flip in far]
    column = join(head[0], rest, heads)
    run = functools.partial(run, spread_own(column, lax.axis_size("off")))
    carry = run((), [column], False)
    first = join(head[1], rests[0], carry[2])
    carry = run(carry, [first], False)
    others = [join(h, r, carry[2]) for h, r in zip(head[2:], rests[1:])]
    twins = [flipped(block, "blk", 1) for block in [column, first] + others]
    carry = run(carry, others + twins[:2], not others)
    return run(carry, twins[2:], True) if others else carry


def by_shifts(local, window, run):
    ranges = lax.axis_size("off")
    column = assemble([shifted(local, "off", -k) for k in range(ranges - 1, 0, -1)] + [local])
    group = column[None]
    while group.shape[0] < window:
        held = group.shape[0]
        more = shifted(group[: min(held, window - held)], "blk", -held)
        group = jnp.concatenate([group, more], axis=0)
    return run(spread_own(column, ranges), (), [group], True)


def body(coefficients):
    count, ranges = lax.axis_size("blk"), lax.axis_size("off")
    window = ranges * min(8, count // ranges)
    tables = angle_tables(coefficients.shape[2])
    flips = window == count and count > 2 and ranges > 1
    if flips and is_power_of_two(count) and is_power_of_two(ranges):
        stage = functools.partial(filter_stage, tables, lambda place, k: place ^ k)
        return by_flips(coefficients, stage)
    stage = functools.partial(filter_stage, tables, lambda place, k: (place + k) % ranges)
    return by_shifts(coefficients, window, stage)


def solution(mesh):
    return jax.shard_map(
        body,
        mesh=mesh,
        in_specs=(P("blk", "off", None),),
        out_specs=(P(("blk", "off"), None, None), P(("blk", "off"))),
        check_vma=False,
    )
```

```python
import functools
import math

import jax
import jax.numpy as jnp
import numpy as np
from jax import lax
from jax.experimental import pallas as pl
from jax.experimental.pallas import tpu as pltpu
from jax.sharding import PartitionSpec as P

epsilon = 1e-06
concentration = 40.0


def split(array):
    high = array.astype(jnp.bfloat16)
    return high, (array - high.astype(jnp.float32)).astype(jnp.bfloat16)


def angle_tables(angular):
    half = angular // 2
    product = np.outer(np.arange(half), np.arange(angular)) % angular
    phase = product.astype(np.float32) * np.float32(2.0 * math.pi / angular)
    real, imag = np.cos(phase), -np.sin(phase)
    forward = np.concatenate([real, real, imag, -imag], axis=0).astype(np.float32)
    high = forward.astype(jnp.bfloat16)
    low = (forward - high.astype(np.float32)).astype(jnp.bfloat16)
    return (
        np.concatenate([high, low], axis=1),
        np.ascontiguousarray(np.concatenate([high.T, high.T], axis=0)),
        np.ascontiguousarray(low.T),
    )


def is_power_of_two(n):
    return n & (n - 1) == 0


def moved(array, axis, pairs):
    return lax.ppermute(array, axis, pairs)


def flipped(array, axis, by):
    return moved(array, axis, [(i, i ^ by) for i in range(lax.axis_size(axis))])


def shifted(array, axis, by):
    count = lax.axis_size(axis)
    return moved(array, axis, [(i, (i + by) % count) for i in range(count)])


def vmem():
    return pl.BlockSpec(memory_space=pltpu.VMEM)


def small_kernel(kernel, outs, count, name, limit, scratch=(), cycles=1000):
    return pl.pallas_call(
        kernel,
        out_shape=outs,
        in_specs=[vmem()] * count,
        out_specs=jax.tree.map(lambda _: vmem(), outs),
        scratch_shapes=scratch,
        compiler_params=pltpu.CompilerParams(vmem_limit_bytes=limit),
        cost_estimate=pl.CostEstimate(flops=cycles * 1024, bytes_accessed=0, transcendentals=0),
        name=name,
    )


def radial_first(source, wide, out, start):
    images, depth, angular = source.shape
    wide[...] = source[...].astype(jnp.float32).reshape(images * depth, angular)
    for r in range(depth):
        out[start + r] = wide[pl.ds(r, images, stride=depth), :].astype(out.dtype)


def spread_kernel(ranges, column, direct_own, swapped_own, own_inverse, wide):
    radial, images, angular = column.shape
    rows = images // ranges
    first = lax.axis_index("off") * rows

    def step(r, squares):
        wide[r] = column[r].astype(jnp.float32)
        new = []
        for i in range(rows):
            row = wide[r, pl.ds(first + i, 1), :]
            direct_own[i, r] = jnp.broadcast_to(row, (8, angular))
            swapped_own[i, r] = jnp.broadcast_to(pltpu.roll(row, angular // 2, 1), (8, angular))
            new.append(squares[i] + row * row)
        return tuple(new)

    zero = jnp.zeros((1, angular), jnp.float32)
    squares = lax.fori_loop(0, radial, step, (zero,) * rows, unroll=8)
    for i in range(rows):
        total = jnp.sum(squares[i], axis=1, keepdims=True) + epsilon
        own_inverse[i : i + 1, :] = jnp.broadcast_to(lax.rsqrt(total), (1, angular))


def spread_own(column, ranges):
    radial, images, angular = column.shape
    rows = images // ranges
    tiles = jax.ShapeDtypeStruct((rows, radial, 8, angular), jnp.float32)
    return small_kernel(
        functools.partial(spread_kernel, ranges),
        (tiles, tiles, jax.ShapeDtypeStruct((rows, angular), jnp.float32)),
        1,
        "spread",
        1 << 22,
        [pltpu.VMEM((radial, images, angular), jnp.float32)],
        1000,
    )(column)


def fold(tiles):
    rows = tiles[0].shape[0]
    number = lax.broadcasted_iota(jnp.int32, tiles[0].shape, 0)
    step = 1
    while step < rows:
        low = (number // step) % 2 == 0
        tiles = [
            jnp.where(low, a, b) + pltpu.roll(jnp.where(low, b, a), step, 0)
            for a, b in zip(tiles[::2], tiles[1::2])
        ]
        step *= 2
    return tiles[0]


def filter_kernel(ranges, slice_place, count, is_first, is_last, *refs):
    forward, backward, backward_low, direct_own, swapped_own, own_inverse, *refs = refs
    groups, refs = refs[:count], refs[count:]
    if not is_first:
        real_before, imag_before, degree_before, *refs = refs
    if is_last:
        out, log_degree, real_sum, imag_sum, *refs = refs
    else:
        real_sum, imag_sum, degrees, *refs = refs
    terms, norms, real_w, imag_w = refs
    _, radial, images, angular = groups[0].shape
    half = angular // 2
    rows = images // ranges
    depth = radial // ranges
    place = lax.axis_index("off")
    f32 = jnp.float32
    partners = images * sum(g.shape[0] for g in groups)

    def each_block(do, carry):
        start = 0
        for group in groups:
            blocks = group.shape[0]
            if blocks == 1:
                carry = do(group, 0, start, carry)
            else:

                def one(b, c, group=group, start=start):
                    return do(group, b, pl.multiple_of(start + b * images, images), c)

                carry = lax.fori_loop(0, blocks, one, carry)
            start += blocks * images
        return carry

    def cross(group, b, start, carry):
        def step(r, sums):
            direct, mixed, square = sums
            x = group[b, r].astype(f32).reshape(images // 8, 8, angular)
            direct = tuple(direct[i] + direct_own[i, r][None] * x for i in range(rows))
            mixed = tuple(mixed[i] + swapped_own[i, r][None] * x for i in range(rows))
            return direct, mixed, square + x * x

        zero = jnp.zeros((images // 8, 8, angular), f32)
        direct, mixed, square = lax.fori_loop(
            0, radial, step, ((zero,) * rows, (zero,) * rows, zero), unroll=True
        )
        for i in range(rows):
            at = pl.ds(i * partners + start, images)
            terms[at, :angular] = direct[i].reshape(images, angular)
            terms[at, angular:] = mixed[i].reshape(images, angular)
        norms[pl.ds(start, images), :] = square.reshape(images, angular)
        return carry

    each_block(cross, 0)

    high, low = split(terms[...])
    both = jnp.dot(high, forward[...], preferred_element_type=f32)
    rest = jnp.dot(low, forward[:, :angular], preferred_element_type=f32)
    correlation = both[:, :angular] + (both[:, angular:] + rest)
    inverse = lax.rsqrt(jnp.sum(norms[...], axis=1, keepdims=True) + epsilon) * concentration
    weights = []
    for i in range(rows):
        exponent = correlation[i * partners : (i + 1) * partners] * own_inverse[i : i + 1] * inverse
        weight = jnp.exp(exponent)
        if is_first:
            numbers = lax.broadcasted_iota(jnp.int32, (partners, angular), 0)
            weight = jnp.where(numbers == place * rows + i, 0.0, weight)
        weights.append(weight)
    high, low = split(jnp.concatenate(weights, axis=0))
    spectral = jnp.dot(jnp.concatenate([high, low], axis=1), backward[...], preferred_element_type=f32)
    spectral = spectral + jnp.dot(high, backward_low[...], preferred_element_type=f32)
    scales = []
    for i in range(rows):
        part = spectral[i * partners : (i + 1) * partners]
        degree = jnp.sum(part[:, :angular], axis=0, keepdims=True)
        if not is_first:
            degree = degree + degree_before[i : i + 1]
        if is_last:
            scales.append(1.0 / degree[:, :1])
            log_degree[i] = jnp.log(degree)[0, 0]
        else:
            degrees[i : i + 1, :] = degree
        real_w[i] = part[:, :angular].astype(jnp.bfloat16).astype(f32)
        imag_w[i] = part[:, angular:].astype(jnp.bfloat16).astype(f32)

    def filtered(pair, carry):
        places = (2 * pair, 2 * pair + 1)
        if is_first:
            zero = jnp.zeros((8, angular), f32)
            start_sums = (((zero,) * rows, (zero,) * rows),) * 2
        else:
            start_sums = tuple(
                (
                    tuple(real_before[i, r] for i in range(rows)),
                    tuple(imag_before[i, r] for i in range(rows)),
                )
                for r in places
            )

        def accumulate(group, b, start, sums):
            new = [(list(s[0]), list(s[1])) for s in sums]
            xs = [group[b, r].astype(f32) for r in places]
            for v in range(images // 8):
                for i in range(rows):
                    real = real_w[i, pl.ds(start + 8 * v, 8), :]
                    imag = imag_w[i, pl.ds(start + 8 * v, 8), :]
                    for n in range(2):
                        x = xs[n][8 * v : 8 * v + 8]
                        new[n][0][i] = new[n][0][i] + real * x
                        new[n][1][i] = new[n][1][i] + imag * x
            return tuple((tuple(a), tuple(b)) for a, b in new)

        totals = each_block(accumulate, start_sums)
        for n in range(2):
            for i in range(rows):
                real_sum[i, places[n]] = totals[n][0][i]
                imag_sum[i, places[n]] = totals[n][1][i]
        return carry

    lax.fori_loop(0, radial // 2, filtered, 0, unroll=True)

    if is_last:
        for k in range(ranges):
            for part in range(depth // 8):
                at = k * depth + 8 * part
                target = slice_place(place, k) * depth + 8 * part
                for i in range(rows):
                    real = fold([real_sum[i, at + n] for n in range(8)])
                    imag = fold([imag_sum[i, at + n] for n in range(8)])
                    total = real + pltpu.roll(imag, half, 1)
                    out[i, pl.ds(pl.multiple_of(target, 8), 8), :] = total * scales[i]


def filter_stage(tables, slice_place, own, carry, groups, is_last):
    ranges = lax.axis_size("off")
    groups = [g.reshape(-1, *g.shape[-3:]) for g in groups]
    _, radial, images, angular = groups[0].shape
    rows = images // ranges
    f32 = jnp.float32
    sums = jax.ShapeDtypeStruct((rows, radial, 8, angular), f32)
    partners = images * sum(g.shape[0] for g in groups)
    scratch = [
        pltpu.VMEM((rows * partners, 2 * angular), f32),
        pltpu.VMEM((partners, angular), f32),
        pltpu.VMEM((rows, partners, angular), f32),
        pltpu.VMEM((rows, partners, angular), f32),
    ]
    if is_last:
        outs = (
            jax.ShapeDtypeStruct((rows, radial, angular), f32),
            jax.ShapeDtypeStruct((rows,), f32),
        )
        out_specs = (vmem(), pl.BlockSpec(memory_space=pltpu.SMEM))
        scratch = [pltpu.VMEM(sums.shape, f32)] * 2 + scratch
    else:
        outs = (sums, sums, jax.ShapeDtypeStruct((rows, angular), f32))
        out_specs = (vmem(),) * 3
    operands = (*tables, *own, *groups, *carry)
    return pl.pallas_call(
        functools.partial(filter_kernel, ranges, slice_place, len(groups), not carry, is_last),
        out_shape=outs,
        in_specs=[vmem()] * len(operands),
        out_specs=out_specs,
        scratch_shapes=scratch,
        compiler_params=pltpu.CompilerParams(
            vmem_limit_bytes=(40 if partners > 8 * images else 8) << 20
        ),
        cost_estimate=pl.CostEstimate(
            flops=4 * partners * radial * 1024 * rows, bytes_accessed=0, transcendentals=0
        ),
        name="filter",
    )(*operands)


def assemble_kernel(*refs):
    *slices, out, wide = refs
    depth = slices[0].shape[1]
    for k, piece in enumerate(slices[::-1]):
        radial_first(piece, wide, out, k * depth)


def assemble(slices):
    images, depth, angular = slices[0].shape
    whole = jax.ShapeDtypeStruct((len(slices) * depth, images, angular), slices[0].dtype)
    wide = [pltpu.VMEM((images * depth, angular), jnp.float32)]
    return small_kernel(assemble_kernel, whole, len(slices), "assemble", 1 << 21, wide, 100)(*slices)


def join_kernel(first, rest, token, out):
    depth = first.shape[0]
    out[:depth] = first[...]
    out[depth:] = rest[...]


def join(first, rest, token):
    depth, images, angular = rest.shape
    whole = jax.ShapeDtypeStruct((first.shape[0] + depth, images, angular), rest.dtype)
    return small_kernel(join_kernel, whole, 3, "join", 1 << 21, (), 100)(first, rest, token)


def by_flips(local, run):
    depth = local.shape[1]
    far = range(lax.axis_size("blk") - 2, 0, -2)
    slices = [flipped(local, "off", k) for k in range(lax.axis_size("off") - 1, 0, -1)]
    heads = assemble([flipped(local, "blk", flip) for flip in far] + [local])
    head = [heads[n * depth : (n + 1) * depth] for n in range(len(far) + 1)]
    head = head[:1] + head[:0:-1]
    rest = assemble(slices)
    rests = [flipped(rest, "blk", flip) for flip in far]
    column = join(head[0], rest, heads)
    run = functools.partial(run, spread_own(column, lax.axis_size("off")))
    carry = run((), [column], False)
    first = join(head[1], rests[0], carry[2])
    carry = run(carry, [first], False)
    others = [join(h, r, carry[2]) for h, r in zip(head[2:], rests[1:])]
    twins = [flipped(block, "blk", 1) for block in [column, first] + others]
    carry = run(carry, twins[:2] + others, not others)
    return run(carry, twins[2:], True) if others else carry


def by_shifts(local, window, run):
    ranges = lax.axis_size("off")
    column = assemble([shifted(local, "off", -k) for k in range(ranges - 1, 0, -1)] + [local])
    group = column[None]
    while group.shape[0] < window:
        held = group.shape[0]
        more = shifted(group[: min(held, window - held)], "blk", -held)
        group = jnp.concatenate([group, more], axis=0)
    return run(spread_own(column, ranges), (), [group], True)


def body(coefficients):
    count, ranges = lax.axis_size("blk"), lax.axis_size("off")
    window = ranges * min(8, count // ranges)
    tables = angle_tables(coefficients.shape[2])
    flips = window == count and count > 2 and ranges > 1
    if flips and is_power_of_two(count) and is_power_of_two(ranges):
        stage = functools.partial(filter_stage, tables, lambda place, k: place ^ k)
        return by_flips(coefficients, stage)
    stage = functools.partial(filter_stage, tables, lambda place, k: (place + k) % ranges)
    return by_shifts(coefficients, window, stage)


def solution(mesh):
    return jax.shard_map(
        body,
        mesh=mesh,
        in_specs=(P("blk", "off", None),),
        out_specs=(P(("blk", "off"), None, None), P(("blk", "off"))),
        check_vma=False,
    )
```

```python
import functools
import math

import jax
import jax.numpy as jnp
import numpy as np
from jax import lax
from jax.experimental import pallas as pl
from jax.experimental.pallas import tpu as pltpu
from jax.sharding import PartitionSpec as P

epsilon = 1e-06
concentration = 40.0


def split(array):
    high = array.astype(jnp.bfloat16)
    return high, (array - high.astype(jnp.float32)).astype(jnp.bfloat16)


def angle_tables(angular):
    half = angular // 2
    product = np.outer(np.arange(half), np.arange(angular)) % angular
    phase = product.astype(np.float32) * np.float32(2.0 * math.pi / angular)
    real, imag = np.cos(phase), -np.sin(phase)
    forward = np.concatenate([real, real, imag, -imag], axis=0).astype(np.float32)
    high = forward.astype(jnp.bfloat16)
    low = (forward - high.astype(np.float32)).astype(jnp.bfloat16)
    return (
        np.concatenate([high, low], axis=1),
        np.ascontiguousarray(np.concatenate([high.T, high.T], axis=0)),
        np.ascontiguousarray(low.T),
    )


def is_power_of_two(n):
    return n & (n - 1) == 0


def moved(array, axis, pairs):
    return lax.ppermute(array, axis, pairs)


def flipped(array, axis, by):
    return moved(array, axis, [(i, i ^ by) for i in range(lax.axis_size(axis))])


def shifted(array, axis, by):
    count = lax.axis_size(axis)
    return moved(array, axis, [(i, (i + by) % count) for i in range(count)])


def vmem():
    return pl.BlockSpec(memory_space=pltpu.VMEM)


def small_kernel(kernel, outs, count, name, limit, scratch=(), cycles=1000):
    return pl.pallas_call(
        kernel,
        out_shape=outs,
        in_specs=[vmem()] * count,
        out_specs=jax.tree.map(lambda _: vmem(), outs),
        scratch_shapes=scratch,
        compiler_params=pltpu.CompilerParams(vmem_limit_bytes=limit),
        cost_estimate=pl.CostEstimate(flops=cycles * 1024, bytes_accessed=0, transcendentals=0),
        name=name,
    )


def radial_first(source, wide, out, start):
    images, depth, angular = source.shape
    wide[...] = source[...].astype(jnp.float32).reshape(images * depth, angular)
    for r in range(depth):
        out[start + r] = wide[pl.ds(r, images, stride=depth), :].astype(out.dtype)


def spread_kernel(ranges, column, direct_own, swapped_own, own_inverse, wide):
    radial, images, angular = column.shape
    rows = images // ranges
    first = lax.axis_index("off") * rows

    def step(r, squares):
        wide[r] = column[r].astype(jnp.float32)
        new = []
        for i in range(rows):
            row = wide[r, pl.ds(first + i, 1), :]
            direct_own[i, r] = jnp.broadcast_to(row, (8, angular))
            swapped_own[i, r] = jnp.broadcast_to(pltpu.roll(row, angular // 2, 1), (8, angular))
            new.append(squares[i] + row * row)
        return tuple(new)

    zero = jnp.zeros((1, angular), jnp.float32)
    squares = lax.fori_loop(0, radial, step, (zero,) * rows, unroll=8)
    for i in range(rows):
        total = jnp.sum(squares[i], axis=1, keepdims=True) + epsilon
        own_inverse[i : i + 1, :] = jnp.broadcast_to(lax.rsqrt(total), (1, angular))


def spread_own(column, ranges):
    radial, images, angular = column.shape
    rows = images // ranges
    tiles = jax.ShapeDtypeStruct((rows, radial, 8, angular), jnp.float32)
    return small_kernel(
        functools.partial(spread_kernel, ranges),
        (tiles, tiles, jax.ShapeDtypeStruct((rows, angular), jnp.float32)),
        1,
        "spread",
        1 << 22,
        [pltpu.VMEM((radial, images, angular), jnp.float32)],
        1000,
    )(column)


def fold(tiles):
    rows = tiles[0].shape[0]
    number = lax.broadcasted_iota(jnp.int32, tiles[0].shape, 0)
    step = 1
    while step < rows:
        low = (number // step) % 2 == 0
        tiles = [
            jnp.where(low, a, b) + pltpu.roll(jnp.where(low, b, a), step, 0)
            for a, b in zip(tiles[::2], tiles[1::2])
        ]
        step *= 2
    return tiles[0]


def filter_kernel(ranges, slice_place, count, is_first, is_last, *refs):
    forward, backward, backward_low, direct_own, swapped_own, own_inverse, *refs = refs
    groups, refs = refs[:count], refs[count:]
    if not is_first:
        real_before, imag_before, degree_before, *refs = refs
    if is_last:
        out, log_degree, real_sum, imag_sum, *refs = refs
    else:
        real_sum, imag_sum, degrees, *refs = refs
    terms, norms, real_w, imag_w = refs
    _, radial, images, angular = groups[0].shape
    half = angular // 2
    rows = images // ranges
    depth = radial // ranges
    place = lax.axis_index("off")
    f32 = jnp.float32
    partners = images * sum(g.shape[0] for g in groups)

    def each_block(do, carry):
        start = 0
        for group in groups:
            blocks = group.shape[0]
            if blocks == 1:
                carry = do(group, 0, start, carry)
            else:

                def one(b, c, group=group, start=start):
                    return do(group, b, pl.multiple_of(start + b * images, images), c)

                carry = lax.fori_loop(0, blocks, one, carry)
            start += blocks * images
        return carry

    def cross(group, b, start, carry):
        def step(r, sums):
            direct, mixed, square = sums
            x = group[b, r].astype(f32).reshape(images // 8, 8, angular)
            direct = tuple(direct[i] + direct_own[i, r][None] * x for i in range(rows))
            mixed = tuple(mixed[i] + swapped_own[i, r][None] * x for i in range(rows))
            return direct, mixed, square + x * x

        zero = jnp.zeros((images // 8, 8, angular), f32)
        direct, mixed, square = lax.fori_loop(
            0, radial, step, ((zero,) * rows, (zero,) * rows, zero), unroll=True
        )
        for i in range(rows):
            at = pl.ds(i * partners + start, images)
            terms[at, :angular] = direct[i].reshape(images, angular)
            terms[at, angular:] = mixed[i].reshape(images, angular)
        norms[pl.ds(start, images), :] = square.reshape(images, angular)
        return carry

    each_block(cross, 0)

    high, low = split(terms[...])
    both = jnp.dot(high, forward[...], preferred_element_type=f32)
    rest = jnp.dot(low, forward[:, :angular], preferred_element_type=f32)
    correlation = both[:, :angular] + (both[:, angular:] + rest)
    inverse = lax.rsqrt(jnp.sum(norms[...], axis=1, keepdims=True) + epsilon) * concentration
    weights = []
    for i in range(rows):
        exponent = correlation[i * partners : (i + 1) * partners] * own_inverse[i : i + 1] * inverse
        weight = jnp.exp(exponent)
        if is_first:
            numbers = lax.broadcasted_iota(jnp.int32, (partners, angular), 0)
            weight = jnp.where(numbers == place * rows + i, 0.0, weight)
        weights.append(weight)
    high, low = split(jnp.concatenate(weights, axis=0))
    spectral = jnp.dot(jnp.concatenate([high, low], axis=1), backward[...], preferred_element_type=f32)
    spectral = spectral + jnp.dot(high, backward_low[...], preferred_element_type=f32)
    scales = []
    for i in range(rows):
        part = spectral[i * partners : (i + 1) * partners]
        degree = jnp.sum(part[:, :angular], axis=0, keepdims=True)
        if not is_first:
            degree = degree + degree_before[i : i + 1]
        if is_last:
            scales.append(1.0 / degree[:, :1])
            log_degree[i] = jnp.log(degree)[0, 0]
        else:
            degrees[i : i + 1, :] = degree
        real_w[i] = part[:, :angular].astype(jnp.bfloat16).astype(f32)
        imag_w[i] = part[:, angular:].astype(jnp.bfloat16).astype(f32)

    def filtered(pair, carry):
        places = (2 * pair, 2 * pair + 1)
        if is_first:
            zero = jnp.zeros((8, angular), f32)
            start_sums = (((zero,) * rows, (zero,) * rows),) * 2
        else:
            start_sums = tuple(
                (
                    tuple(real_before[i, r] for i in range(rows)),
                    tuple(imag_before[i, r] for i in range(rows)),
                )
                for r in places
            )

        def accumulate(group, b, start, sums):
            new = [(list(s[0]), list(s[1])) for s in sums]
            xs = [group[b, r].astype(f32) for r in places]
            for v in range(images // 8):
                for i in range(rows):
                    real = real_w[i, pl.ds(start + 8 * v, 8), :]
                    imag = imag_w[i, pl.ds(start + 8 * v, 8), :]
                    for n in range(2):
                        x = xs[n][8 * v : 8 * v + 8]
                        new[n][0][i] = new[n][0][i] + real * x
                        new[n][1][i] = new[n][1][i] + imag * x
            return tuple((tuple(a), tuple(b)) for a, b in new)

        totals = each_block(accumulate, start_sums)
        for n in range(2):
            for i in range(rows):
                real_sum[i, places[n]] = totals[n][0][i]
                imag_sum[i, places[n]] = totals[n][1][i]
        return carry

    lax.fori_loop(0, radial // 2, filtered, 0, unroll=True)

    if is_last:
        for k in range(ranges):
            for part in range(depth // 8):
                at = k * depth + 8 * part
                target = slice_place(place, k) * depth + 8 * part
                for i in range(rows):
                    real = fold([real_sum[i, at + n] for n in range(8)])
                    imag = fold([imag_sum[i, at + n] for n in range(8)])
                    total = real + pltpu.roll(imag, half, 1)
                    out[i, pl.ds(pl.multiple_of(target, 8), 8), :] = total * scales[i]


def filter_stage(tables, slice_place, own, carry, groups, is_last):
    ranges = lax.axis_size("off")
    groups = [g.reshape(-1, *g.shape[-3:]) for g in groups]
    _, radial, images, angular = groups[0].shape
    rows = images // ranges
    f32 = jnp.float32
    sums = jax.ShapeDtypeStruct((rows, radial, 8, angular), f32)
    partners = images * sum(g.shape[0] for g in groups)
    scratch = [
        pltpu.VMEM((rows * partners, 2 * angular), f32),
        pltpu.VMEM((partners, angular), f32),
        pltpu.VMEM((rows, partners, angular), f32),
        pltpu.VMEM((rows, partners, angular), f32),
    ]
    if is_last:
        outs = (
            jax.ShapeDtypeStruct((rows, radial, angular), f32),
            jax.ShapeDtypeStruct((rows,), f32),
        )
        out_specs = (vmem(), pl.BlockSpec(memory_space=pltpu.SMEM))
        scratch = [pltpu.VMEM(sums.shape, f32)] * 2 + scratch
    else:
        outs = (sums, sums, jax.ShapeDtypeStruct((rows, angular), f32))
        out_specs = (vmem(),) * 3
    operands = (*tables, *own, *groups, *carry)
    return pl.pallas_call(
        functools.partial(filter_kernel, ranges, slice_place, len(groups), not carry, is_last),
        out_shape=outs,
        in_specs=[vmem()] * len(operands),
        out_specs=out_specs,
        scratch_shapes=scratch,
        compiler_params=pltpu.CompilerParams(
            vmem_limit_bytes=(40 if partners > 8 * images else 8) << 20
        ),
        cost_estimate=pl.CostEstimate(
            flops=4 * partners * radial * 1024 * rows, bytes_accessed=0, transcendentals=0
        ),
        name="filter",
    )(*operands)


def assemble_kernel(places, *refs):
    *slices, out, wide = refs
    depth = slices[0].shape[1]
    for place, piece in zip(places, slices):
        radial_first(piece, wide, out, place * depth)


def assemble(slices, places=None):
    places = places or range(len(slices) - 1, -1, -1)
    kernel = functools.partial(assemble_kernel, tuple(places))
    images, depth, angular = slices[0].shape
    whole = jax.ShapeDtypeStruct((len(slices) * depth, images, angular), slices[0].dtype)
    wide = [pltpu.VMEM((images * depth, angular), jnp.float32)]
    return small_kernel(kernel, whole, len(slices), "assemble", 1 << 21, wide, 100)(*slices)


def join_kernel(first, rest, token, out):
    depth = first.shape[0]
    out[:depth] = first[...]
    out[depth:] = rest[...]


def join(first, rest, token):
    depth, images, angular = rest.shape
    whole = jax.ShapeDtypeStruct((first.shape[0] + depth, images, angular), rest.dtype)
    return small_kernel(join_kernel, whole, 3, "join", 1 << 21, (), 100)(first, rest, token)


def by_flips(local, run):
    depth = local.shape[1]
    far = range(lax.axis_size("blk") - 2, 0, -2)
    steps = list(range(lax.axis_size("off") - 1, 0, -1))
    steps[:2] = steps[1::-1]
    slices = [flipped(local, "off", k) for k in steps]
    heads = assemble([flipped(local, "blk", flip) for flip in far] + [local])
    head = [heads[n * depth : (n + 1) * depth] for n in range(len(far) + 1)]
    head = head[:1] + head[:0:-1]
    rest = assemble(slices, [k - 1 for k in steps])
    rests = [flipped(rest, "blk", flip) for flip in far]
    column = join(head[0], rest, heads)
    run = functools.partial(run, spread_own(column, lax.axis_size("off")))
    carry = run((), [column], False)
    first = join(head[1], rests[0], carry[2])
    carry = run(carry, [first], False)
    others = [join(h, r, carry[2]) for h, r in zip(head[2:], rests[1:])]
    twins = [flipped(block, "blk", 1) for block in [column, first] + others]
    carry = run(carry, twins[:2] + others, not others)
    return run(carry, twins[2:], True) if others else carry


def by_shifts(local, window, run):
    ranges = lax.axis_size("off")
    column = assemble([shifted(local, "off", -k) for k in range(ranges - 1, 0, -1)] + [local])
    group = column[None]
    while group.shape[0] < window:
        held = group.shape[0]
        more = shifted(group[: min(held, window - held)], "blk", -held)
        group = jnp.concatenate([group, more], axis=0)
    return run(spread_own(column, ranges), (), [group], True)


def body(coefficients):
    count, ranges = lax.axis_size("blk"), lax.axis_size("off")
    window = ranges * min(8, count // ranges)
    tables = angle_tables(coefficients.shape[2])
    flips = window == count and count > 2 and ranges > 1
    if flips and is_power_of_two(count) and is_power_of_two(ranges):
        stage = functools.partial(filter_stage, tables, lambda place, k: place ^ k)
        return by_flips(coefficients, stage)
    stage = functools.partial(filter_stage, tables, lambda place, k: (place + k) % ranges)
    return by_shifts(coefficients, window, stage)


def solution(mesh):
    return jax.shard_map(
        body,
        mesh=mesh,
        in_specs=(P("blk", "off", None),),
        out_specs=(P(("blk", "off"), None, None), P(("blk", "off"))),
        check_vma=False,
    )
```
